256 devices in a mesh: row: 16 (over y, z_lo, core), col: 16 (over x, z_hi).
Axes of the slice: x: 4, y: 4, z: 8 (z_hi: 4, z_lo: 2; z = z_hi * 2 + z_lo), core: 2. Of those that a mesh axis runs over, the one named last changes fastest.
Arguments:
- coeffs: float32 [8192, 8192], P('row', 'col'), may hold values from -8 to 8, as said below
- features: float32 [8192, 512], P('row'), may hold values from -0.6 to 0.6
- factors: float32 [8192, 256], P('row'), may hold values from -1.8 to 1.8
Outputs:
- grad_coeffs: float32 [8192, 8192], P('row', 'col')
- grad_features: float32 [8192, 512], P('row', 'col')
The draws below stay inside these ranges and needn't reach their ends.
Inputs may be any that keep to these rules, and one draw needn't show every extreme that they name: `coeffs`: real coefficients.
All inputs are finite; a program needn't handle non-finite values.
Results may differ from the reference program's by a relative error of at most 0.0003.
Values sent between devices are 32-bit elements; how exact they have to be, the bound alone decides.
A program may use at most 64 MiB of HBM per device.

```python
import math
import jax
import jax.numpy as jnp
from jax import lax

F = 512
K = 256
SAMPLES = 8192


def draw_coeffs(key, part):
    first, second, third = jax.random.split(jax.random.fold_in(key, 17), 3)
    shape = (SAMPLES, SAMPLES)
    background = jax.random.normal(first, shape, jnp.float32)
    picked = jax.random.bernoulli(second, 8.0 / SAMPLES, shape)
    paired = jnp.logical_or(picked, picked.T)
    heavy = jax.random.uniform(third, shape, jnp.float32, -1.5, 1.5)
    values = background * (3.0 * SAMPLES ** (-0.5)) + jnp.where(paired, heavy, 0.0)
    return values.astype(jnp.float32)


def block_scale(stream_key, dims, cuts, low, high):
    factor_of, own = 1.0, jax.random.fold_in(stream_key, 6)
    for dim, parts in cuts:
        steps = jnp.exp(jax.random.uniform(jax.random.fold_in(own, dim), (parts,), jnp.float32, low / len(cuts), high / len(cuts)))
        factor_of = factor_of * jnp.repeat(steps, dims[dim] // parts).reshape([-1 if axis == dim else 1 for axis in range(len(dims))])
    return factor_of


def normal_values(key, extent, deviation, most, cuts=(), kind=jnp.bfloat16):
    array = deviation * jax.random.normal(key, extent, jnp.float32)
    if cuts:
        array = array * block_scale(key, extent, cuts, -0.22, 0.18)
    return jnp.clip(array, -most, most).astype(kind)


def setup_inputs(seed: int = 0) -> dict:
    arg_keys = jax.random.split(jax.random.key(seed), 4)
    coeffs = draw_coeffs(jax.random.fold_in(arg_keys[3], 71), 0)
    features = normal_values(arg_keys[1], (SAMPLES, F), 0.1, 0.6, ((0, 16),), jnp.float32)
    factors = normal_values(arg_keys[2], (SAMPLES, K), 0.3, 1.8, ((0, 16),), jnp.float32)
    return dict(coeffs=coeffs, features=features, factors=factors)


def reference(coeffs, features, factors):
    highest = lax.Precision.HIGHEST
    residual = jnp.dot(coeffs, features, precision=highest, preferred_element_type=jnp.float32) - features
    grad_features = jnp.dot(coeffs.T, residual, precision=highest, preferred_element_type=jnp.float32) - residual
    block_rows = math.gcd(SAMPLES, 512)

    def one_block(row_start):
        row_start = row_start.astype(jnp.int32)
        rows = lax.dynamic_slice_in_dim(coeffs, row_start, block_rows, 0)
        mirrored = lax.dynamic_slice_in_dim(coeffs, row_start, block_rows, 1).T
        symmetric = 0.5 * (rows * rows + mirrored * mirrored)
        own_factors = lax.dynamic_slice_in_dim(factors, row_start, block_rows, 0)
        relation = symmetric - jnp.dot(own_factors, factors.T, precision=highest, preferred_element_type=jnp.float32)
        own_residual = lax.dynamic_slice_in_dim(residual, row_start, block_rows, 0)
        outer = jnp.dot(own_residual, features.T, precision=highest, preferred_element_type=jnp.float32)
        return outer + 2.0 * rows * relation

    starts = jnp.arange(SAMPLES // block_rows, dtype=jnp.int32) * block_rows
    grad_coeffs = lax.map(one_block, starts).reshape(SAMPLES, SAMPLES)
    return grad_coeffs, grad_features
```

```python
import functools

import jax
import jax.numpy as jnp
from jax import lax
from jax.experimental import pallas as pl
from jax.experimental.pallas import tpu as pltpu
from jax.sharding import PartitionSpec as P

F32, BF16 = jnp.float32, jnp.bfloat16
MESH = pl.DeviceIdType.MESH
NN = (((1,), (0,)), ((), ()))
NT = (((1,), (1,)), ((), ()))
S = 32
G = 128


def split(a):
    hi = a.astype(BF16)
    return hi, (a - hi.astype(F32)).astype(BF16)


def dot3(a, b, dims):
    ah, al = a
    bh, bl = b
    dot = functools.partial(lax.dot_general, dimension_numbers=dims, preferred_element_type=F32)
    return dot(ah, bh) + (dot(ah, bl) + dot(al, bh))


def kernel(
    c_ref, z_ref, h_ref, dc_ref, dz_ref,
    zslab, zct, hc, m, ch, cl, pt, ra, sb, rb, rt, tt, rc, se, rd, tot, dzt,
    send, rsend,
    st_sem, m_sem, zg_sem, zc_sem, hg_sem, hcs_sem, ra_sem, rb_sem, ag_sem, rc_sem, rd_sem, fin_sem,
):
    r, c = lax.axis_index("row"), lax.axis_index("col")
    y, zl, co = r // 4, (r // 2) % 2, r % 2
    x, zh = c // 4, c % 4
    swap = r != c
    mate = r + 1 - 2 * co

    def rows(start, size=S):
        return pl.ds(pl.multiple_of(start * S, S), size)

    def row_peer(dy, dz):
        return ((y + dy) % 4) * 4 + ((zl + dz) % 2) * 2 + co

    def row_from(dy, dz):
        return ((y - dy) % 4) * 4 + ((zl - dz) % 2) * 2 + co

    count = [0]
    pending = []

    def copy(src, dst, sem, row, col):
        n = count[0]
        count[0] += 1
        return pltpu.make_async_remote_copy(
            src_ref=src, dst_ref=dst, send_sem=send.at[n], recv_sem=sem,
            device_id={"row": row, "col": col}, device_id_type=MESH,
        )

    def put(src, dst, sem, row, col):
        one = copy(src, dst, sem, row, col)
        one.start()
        pending.append(one)

    def got(dst, sem):
        pltpu.make_async_remote_copy(
            src_ref=dst, dst_ref=dst, send_sem=rsend, recv_sem=sem,
            device_id={"row": mate, "col": c}, device_id_type=MESH,
        ).wait_recv()

    offsets = [(dy, dz) for dy in range(4) for dz in range(2) if (dy, dz) != (0, 0)]

    barrier = pltpu.get_barrier_semaphore()
    peers = [(mate, c)]
    peers += [(row_peer(dy, dz), c) for dy, dz in offsets]
    peers += [(r, ((x + d) % 4) * 4 + zh) for d in range(1, 4)]
    peers += [(r, x * 4 + (zh + d) % 4) for d in range(1, 4)]
    for row, col in peers:
        pl.semaphore_signal(barrier, inc=1, device_id={"row": row, "col": col}, device_id_type=MESH)

    @pl.when(swap)
    def _():
        pl.semaphore_signal(barrier, inc=1, device_id={"row": c, "col": r}, device_id_type=MESH)

    zslab[...] = z_ref[:, pl.ds(pl.multiple_of(x * G, G), G)].T
    pl.semaphore_wait(barrier, len(peers) + swap.astype(jnp.int32))

    mine = zslab.at[rows(zh)]
    first = copy(mine, zct.at[rows(c)], st_sem.at[0], c, r)
    second = copy(h_ref.at[rows(c)], hc.at[rows(c)], st_sem.at[1], c, r)
    third = copy(c_ref, m, m_sem, c, r)

    @pl.when(swap)
    def _():
        first.start()
        second.start()
        third.start()

    @pl.when(jnp.logical_not(swap))
    def _():
        zct[rows(c)] = zslab[rows(zh)]
        hc[rows(c)] = h_ref[rows(c)]

    hi, lo = split(c_ref[...])
    ch[...] = hi
    cl[...] = lo

    def spread(buf, own, across, start):
        put(buf.at[rows(r)], buf.at[rows(r)], across.at[0], mate, c)
        for n, (dy, dz) in enumerate(offsets):
            put(buf.at[rows(r)], buf.at[rows(r)], own.at[n], row_peer(dy, dz), c)

    def forward(buf, own, across):
        for n, (dy, dz) in enumerate(offsets):
            here = buf.at[rows(row_from(dy, dz))]
            got(here, own.at[n])
            put(here, here, across.at[n + 1], mate, c)

    def collect(buf, across):
        got(buf.at[rows(mate)], across.at[0])
        for n, (dy, dz) in enumerate(offsets):
            got(buf.at[rows(row_from(dy, dz) + 1 - 2 * co)], across.at[n + 1])

    @pl.when(swap)
    def _():
        first.wait_recv()

    spread(zct, zg_sem, zc_sem, 0)
    forward(zct, zg_sem, zc_sem)
    collect(zct, zc_sem)

    for d in (1, 2, 3, 0):
        k = (x + d) % 4
        block = pl.ds(pl.multiple_of(k * G, G), G)
        pt[block] = dot3(split(zct[block]), (ch[...], cl[...]), NT)
        if d:
            for j in (1, 2, 3, 0):
                zj = (zh + j) % 4
                put(pt.at[rows(k * 4 + zj)], ra.at[d - 1, rows(zj)], ra_sem.at[d - 1, j], r, k * 4 + zh)
    for j in (1, 2, 3, 0):
        zj = (zh + j) % 4
        for d in range(3):
            got(ra.at[d, rows(zj)], ra_sem.at[d, j])
        total = pt[rows(x * 4 + zj)] + ra[0, rows(zj)] + ra[1, rows(zj)] + ra[2, rows(zj)]
        sb[j] = total
        if j:
            put(sb.at[j], rb.at[j], rb_sem.at[j], r, x * 4 + zj)
    for j in range(1, 4):
        got(rb.at[j], rb_sem.at[j])
    rt[rows(c)] = sb[0] + rb[1] + rb[2] + rb[3] - zslab[rows(zh)]

    own = rt.at[rows(c)]
    for j in range(1, 4):
        put(own, own, ag_sem.at[0, j], r, x * 4 + (zh + j) % 4)
    for d in range(1, 4):
        put(own, own, ag_sem.at[d, 0], r, ((x + d) % 4) * 4 + zh)
    for j in range(1, 4):
        here = rt.at[rows(x * 4 + (zh - j) % 4)]
        got(here, ag_sem.at[0, j])
        for d in range(1, 4):
            put(here, here, ag_sem.at[d, j], r, ((x + d) % 4) * 4 + zh)

    @pl.when(swap)
    def _():
        second.wait_recv()

    spread(hc, hg_sem, hcs_sem, 0)
    forward(hc, hg_sem, hcs_sem)
    collect(hc, hcs_sem)

    @pl.when(swap)
    def _():
        third.wait_recv()

    @pl.when(jnp.logical_not(swap))
    def _():
        m[...] = c_ref[...]

    across = m[...].T
    own_c = c_ref[...]
    symmetric = 0.5 * (own_c * own_c + across * across)
    relation = symmetric - dot3(split(h_ref[...]), split(hc[...]), NT)
    dc_ref[...] = 2.0 * own_c * relation

    slot = y * 2 + zl

    for d in range(4):
        k = (x - d) % 4
        if d:
            for j in range(4):
                got(rt.at[rows(k * 4 + (zh - j) % 4)], ag_sem.at[d, j])
        block = pl.ds(pl.multiple_of(k * G, G), G)
        tt[d] = dot3(split(rt[block]), (ch[...], cl[...]), NN)
        for j in range(2):
            put(tt.at[d, rows(j * 2 + 1 - co)], rc.at[d, j], rc_sem.at[d, j], mate, c)
    sent = []
    for d in range(4):
        k = (x - d) % 4
        for j in range(2):
            got(rc.at[d, j], rc_sem.at[d, j])
            target = k * 4 + j * 2 + co
            here = target == r
            se[d, j] = tt[d, rows(j * 2 + co)] + rc[d, j]
            one = copy(se.at[d, j], rd.at[slot], rd_sem.at[slot], target, c)
            sent.append((here, one))

            @pl.when(here)
            def _(d=d, j=j):
                rd[slot] = se[d, j]

            @pl.when(jnp.logical_not(here))
            def _(one=one):
                one.start()

    dc_ref[...] += dot3(split(rt[...].T), split(zct[...]), NN)

    for s in range(8):

        @pl.when(s != slot)
        def _(s=s):
            got(rd.at[s], rd_sem.at[s])

    tot[...] = ((rd[0] + rd[1]) + (rd[2] + rd[3])) + ((rd[4] + rd[5]) + (rd[6] + rd[7]))
    last = copy(tot, dzt, fin_sem, c, r)

    @pl.when(swap)
    def _():
        last.start()
        last.wait_recv()

    @pl.when(jnp.logical_not(swap))
    def _():
        dzt[...] = tot[...]

    dz_ref[...] = (dzt[...] - rt[rows(c)]).T

    for one in pending:
        one.wait_send()
    for here, one in sent:

        @pl.when(jnp.logical_not(here))
        def _(one=one):
            one.wait_send()

    @pl.when(swap)
    def _():
        for one in (first, second, third, last):
            one.wait_send()


def per_device(coeffs, features, factors):
    n, f = features.shape
    vmem = pl.BlockSpec(memory_space=pltpu.VMEM)
    dma = pltpu.SemaphoreType.DMA
    buf = lambda *shape: pltpu.VMEM(shape, F32)
    return pl.pallas_call(
        kernel,
        out_shape=(
            jax.ShapeDtypeStruct((n, n), F32),
            jax.ShapeDtypeStruct((n, S), F32),
        ),
        in_specs=[vmem] * 3,
        out_specs=(vmem, vmem),
        scratch_shapes=[
            buf(G, n), buf(f, n), buf(n, factors.shape[1]), buf(n, n),
            pltpu.VMEM((n, n), BF16), pltpu.VMEM((n, n), BF16),
            buf(f, n), buf(3, G, n), buf(4, S, n), buf(4, S, n), buf(f, n),
            buf(4, G, n), buf(4, 2, S, n), buf(4, 2, S, n), buf(8, S, n), buf(S, n), buf(S, n),
            dma((96,)), dma(()),
            dma((2,)), dma(()), dma((7,)), dma((8,)), dma((7,)), dma((8,)),
            dma((3, 4)), dma((4,)), dma((4, 4)), dma((4, 2)), dma((8,)), dma(()),
        ],
        compiler_params=pltpu.CompilerParams(
            collective_id=0, has_side_effects=True, vmem_limit_bytes=48 << 20
        ),
    )(coeffs, features, factors)


def solution(mesh):
    in_specs = (P("row", "col"), P("row", None), P("row", None))
    out_specs = (P("row", "col"), P("row", "col"))
    return jax.shard_map(
        per_device, mesh=mesh, in_specs=in_specs, out_specs=out_specs, check_vma=False
    )
```

```python
import functools

import jax
import jax.numpy as jnp
from jax import lax
from jax.experimental import pallas as pl
from jax.experimental.pallas import tpu as pltpu
from jax.sharding import PartitionSpec as P

F32, BF16 = jnp.float32, jnp.bfloat16
MESH = pl.DeviceIdType.MESH
NN = (((1,), (0,)), ((), ()))
NT = (((1,), (1,)), ((), ()))
TP = '0237'
MP = '6789'
HS = '1'
HQ = '6'
HF = '8'
S = 32
G = 128


def split(a):
    hi = a.astype(BF16)
    return hi, (a - hi.astype(F32)).astype(BF16)


def dot3(a, b, dims):
    ah, al = a
    bh, bl = b
    dot = functools.partial(lax.dot_general, dimension_numbers=dims, preferred_element_type=F32)
    return dot(ah, bh) + (dot(ah, bl) + dot(al, bh))


def kernel(
    c_ref, z_ref, h_ref, dc_ref, dz_ref,
    cv, hv, zfirst, zown, zslab, zsub, zct, hc, m, relay, ch, cl, pt, ra, sb, rb, rt, tt, rc, se, rd, tot, dzt,
    send, rsend, in_sem,
    st_sem, m_sem, y_sem, zg_sem, zc_sem, hg_sem, hcs_sem, ra_sem, rb_sem, ag_sem, rc_sem, rd_sem, fin_sem,
):
    r, c = lax.axis_index("row"), lax.axis_index("col")
    y, zl, co = r // 4, (r // 2) % 2, r % 2
    x, zh = c // 4, c % 4
    swap = r != c
    diagonal = x == y
    far = (x - y + 4) % 4 == 2
    mate = r + 1 - 2 * co
    turn = (x + y) % 4

    def rows(start, size=S):
        return pl.ds(pl.multiple_of(start * S, S), size)

    def group(k):
        return pl.ds(pl.multiple_of(k * G, G), G)

    def row_peer(dy, dz):
        return ((y + dy) % 4) * 4 + ((zl + dz) % 2) * 2 + co

    def slice_from(dy, dz, core):
        return rows(((y - dy + x + 4) % 4) * 4 + ((zl + dz) % 2) * 2 + core)

    count = [0]
    pending = []

    def copy(src, dst, sem, row, col):
        n = count[0]
        count[0] += 1
        return pltpu.make_async_remote_copy(
            src_ref=src, dst_ref=dst, send_sem=send.at[n], recv_sem=sem,
            device_id={"row": row, "col": col}, device_id_type=MESH,
        )

    def put(src, dst, sem, row, col):
        one = copy(src, dst, sem, row, col)
        one.start()
        pending.append((None, one))

    def put_if(where, src, dst, sem, row, col):
        one = copy(src, dst, sem, row, col)

        @pl.when(where)
        def _():
            one.start()

        pending.append((where, one))

    def got(dst, sem):
        pltpu.make_async_remote_copy(
            src_ref=dst, dst_ref=dst, send_sem=rsend, recv_sem=sem,
            device_id={"row": mate, "col": c}, device_id_type=MESH,
        ).wait_recv()

    offsets = [(0, 1), (1, 0), (1, 1), (3, 0), (3, 1), (2, 0), (2, 1)]

    lanes = lambda k: pl.ds(pl.multiple_of(k * G, G), G)
    loads = [
        pltpu.make_async_copy(z_ref.at[:, lanes(turn)], zfirst, in_sem.at[0]),
        pltpu.make_async_copy(c_ref, cv, in_sem.at[1]),
        pltpu.make_async_copy(z_ref.at[:, lanes(x)], zown, in_sem.at[2]),
        pltpu.make_async_copy(h_ref, hv, in_sem.at[3]),
    ]
    for one in loads:
        one.start()

    barrier = pltpu.get_barrier_semaphore()

    def greet(row, col):
        pl.semaphore_signal(barrier, inc=1, device_id={"row": row, "col": col}, device_id_type=MESH)

    @pl.when(swap)
    def _():
        greet(c, r)

    @pl.when(diagonal)
    def _():
        greet(((y + 2) % 4) * 4 + zh, r)

    peers = [(mate, c)]
    peers += [(row_peer(dy, dz), c) for dy, dz in offsets]
    peers += [(r, ((x + d) % 4) * 4 + zh) for d in range(1, 4)]
    peers += [(r, x * 4 + (zh + d) % 4) for d in range(1, 4)]
    for row, col in peers:
        greet(row, col)
    loads[0].wait()
    zslab[...] = zfirst[...].T
    pl.semaphore_wait(barrier, len(peers) + swap.astype(jnp.int32) + far.astype(jnp.int32))

    mine = rows(turn * 4 + zh)
    ours = slice_from(0, 0, co)
    first = copy(zslab.at[rows(zh)], zct.at[mine], st_sem.at[0], c, r)
    second = copy(h_ref.at[mine], hc.at[mine], st_sem.at[1], c, r)

    @pl.when(swap)
    def _():
        first.start()

    @pl.when(jnp.logical_not(swap))
    def _():
        zct[mine] = zslab[rows(zh)]

    near = jnp.logical_and(swap, jnp.logical_not(far))
    hop = []

    def mirror_out(i):
        part = pl.ds(i * G, G)
        put_if(near, c_ref.at[part], m.at[part], m_sem.at[i], c, r)
        put_if(far, c_ref.at[part], relay.at[part], y_sem.at[i], c, x * 4 + r % 4)

    def mirror_pass(i):
        part = pl.ds(i * G, G)
        one = copy(relay.at[part], m.at[part], m_sem.at[i], r, ((y + 2) % 4) * 4 + zh)

        @pl.when(diagonal)
        def _():
            got(relay.at[part], y_sem.at[i])
            one.start()

        pending.append((diagonal, one))

    def swap_factors():
        @pl.when(swap)
        def _():
            second.start()

    def point(name):
        if name == HS:
            swap_factors()
        if name == HQ:
            @pl.when(swap)
            def _():
                second.wait_recv()
            spread(hc, hg_sem, hcs_sem)
        if name == HF:
            for n in range(7):
                forward(hc, hg_sem, hcs_sem, n)
        for i in range(4):
            if TP[i] == name:
                mirror_out(i)
        for i in range(4):
            if MP[i] == name:
                mirror_pass(i)

    def spread(buf, own, across):
        put(buf.at[ours], buf.at[ours], across.at[0], mate, c)
        for n, (dy, dz) in enumerate(offsets):
            put(buf.at[ours], buf.at[ours], own.at[n], row_peer(dy, dz), c)

    def forward(buf, own, across, n):
        here = buf.at[slice_from(*offsets[n], co)]
        got(here, own.at[n])
        put(here, here, across.at[n + 1], mate, c)

    def collect(buf, across, n):
        got(buf.at[slice_from(*((0, 0) if n == 0 else offsets[n - 1]), 1 - co)], across.at[n])

    point('0')
    loads[1].wait()
    hi, lo = split(cv[...])
    ch[...] = hi
    cl[...] = lo
    loads[2].wait()
    zsub[...] = zown[...].T

    loads[3].wait()

    @pl.when(jnp.logical_not(swap))
    def _():
        hc[mine] = hv[mine]

    @pl.when(swap)
    def _():
        first.wait_recv()

    spread(zct, zg_sem, zc_sem)
    point('1')

    for step, dy in enumerate((0, 1, 3, 2)):
        for n in ((0,), (1, 2), (3, 4), (5, 6))[step]:
            forward(zct, zg_sem, zc_sem, n)
        for n in ((0, 1), (2, 3), (4, 5), (6, 7))[step]:
            collect(zct, zc_sem, n)
        k = (y - dy + x + 4) % 4
        pt[step] = dot3(split(zct[group(k)]), (ch[...], cl[...]), NT)
        for j in (1, 2, 3, 0):
            zj = (zh + j) % 4
            put_if(k != x, pt.at[step, rows(zj)], ra.at[x, rows(zj)], ra_sem.at[x, j], r, k * 4 + zh)

        @pl.when(k == x)
        def _(step=step):
            ra[x] = pt[step]

        point('2345'[step])


    for j in (1, 2, 3, 0):
        zj = (zh + j) % 4
        for d in range(1, 4):
            source = (x + d) % 4
            got(ra.at[source, rows(zj)], ra_sem.at[source, j])
        total = (ra[0, rows(zj)] + ra[1, rows(zj)]) + (ra[2, rows(zj)] + ra[3, rows(zj)])
        sb[j] = total
        if j:
            put(sb.at[j], rb.at[j], rb_sem.at[j], r, x * 4 + zj)
    point('6')
    for j in range(1, 4):
        got(rb.at[j], rb_sem.at[j])
    rt[rows(c)] = sb[0] + rb[1] + rb[2] + rb[3] - zsub[rows(zh)]

    own = rt.at[rows(c)]
    for j in range(1, 4):
        put(own, own, ag_sem.at[0, j], r, x * 4 + (zh + j) % 4)
    for d in range(1, 4):
        put(own, own, ag_sem.at[d, 0], r, ((x + d) % 4) * 4 + zh)
    point('7')
    for j in range(1, 4):
        here = rt.at[rows(x * 4 + (zh - j + 4) % 4)]
        got(here, ag_sem.at[0, j])
        for d in range(1, 4):
            put(here, here, ag_sem.at[d, j], r, ((x + d) % 4) * 4 + zh)

    point('8')

    slot = y * 2 + zl
    def reduce_row(d):
        k = (x - d + 4) % 4
        for j in range(2):
            got(rc.at[d, j], rc_sem.at[d, j])
            target = k * 4 + j * 2 + co
            se[d, j] = tt[d, rows(j * 2 + co)] + rc[d, j]
            put_if(target != r, se.at[d, j], rd.at[slot], rd_sem.at[slot], target, c)

            @pl.when(target == r)
            def _():
                rd[slot] = se[d, j]

    for d in range(4):
        k = (x - d + 4) % 4
        if d:
            for j in range(4):
                got(rt.at[rows(k * 4 + (zh - j + 4) % 4)], ag_sem.at[d, j])
        tt[d] = dot3(split(rt[group(k)]), (ch[...], cl[...]), NN)
        for j in range(2):
            put(tt.at[d, rows(j * 2 + 1 - co)], rc.at[d, j], rc_sem.at[d, j], mate, c)
        if d == 0:
            for n in range(8):
                collect(hc, hcs_sem, n)
            own_c = cv[...]
            dc_ref[...] = own_c * own_c - 2.0 * dot3(split(hv[...]), split(hc[...]), NT)
        if d:
            reduce_row(d - 1)
        point('9abc'[d])
    reduce_row(3)
    point('d')

    outer = dot3(split(rt[...].T), split(zct[...]), NN)
    dc_ref[...] = outer + cv[...] * dc_ref[...]

    for s in range(8):

        @pl.when(s != slot)
        def _(s=s):
            got(rd.at[s], rd_sem.at[s])

    tot[...] = ((rd[0] + rd[1]) + (rd[2] + rd[3])) + ((rd[4] + rd[5]) + (rd[6] + rd[7]))
    put_if(swap, tot, dzt, fin_sem, c, r)

    @pl.when(swap)
    def _():
        for i in range(4):
            got(m.at[pl.ds(i * G, G)], m_sem.at[i])

    @pl.when(jnp.logical_not(swap))
    def _():
        m[...] = cv[...]

    across = m[...].T
    dc_ref[...] += cv[...] * (across * across)

    @pl.when(swap)
    def _():
        got(dzt, fin_sem)

    @pl.when(jnp.logical_not(swap))
    def _():
        dzt[...] = tot[...]

    dz_ref[...] = (dzt[...] - rt[rows(c)]).T

    for where, one in [(swap, first), (swap, second)] + pending:
        if where is None:
            one.wait_send()
        else:

            @pl.when(where)
            def _(one=one):
                one.wait_send()


def per_device(coeffs, features, factors):
    n, f = features.shape
    k = factors.shape[1]
    vmem = pl.BlockSpec(memory_space=pltpu.VMEM)
    dma = pltpu.SemaphoreType.DMA
    buf = lambda *shape: pltpu.VMEM(shape, F32)
    return pl.pallas_call(
        kernel,
        out_shape=(
            jax.ShapeDtypeStruct((n, n), F32),
            jax.ShapeDtypeStruct((n, S), F32),
        ),
        in_specs=[pl.BlockSpec(memory_space=pl.ANY)] * 3,
        out_specs=(vmem, vmem),
        scratch_shapes=[
            buf(n, n), buf(n, k), buf(n, G), buf(n, G), buf(G, n), buf(G, n), buf(f, n), buf(n, k), buf(n, n), buf(n, n),
            pltpu.VMEM((n, n), BF16), pltpu.VMEM((n, n), BF16),
            buf(4, G, n), buf(4, G, n), buf(4, S, n), buf(4, S, n), buf(f, n),
            buf(4, G, n), buf(4, 2, S, n), buf(4, 2, S, n), buf(8, S, n), buf(S, n), buf(S, n),
            dma((128,)), dma(()), dma((4,)),
            dma((2,)), dma((4,)), dma((4,)), dma((7,)), dma((8,)), dma((7,)), dma((8,)),
            dma((4, 4)), dma((4,)), dma((4, 4)), dma((4, 2)), dma((8,)), dma(()),
        ],
        compiler_params=pltpu.CompilerParams(
            collective_id=0, has_side_effects=True, vmem_limit_bytes=48 << 20
        ),
    )(coeffs, features, factors)


def solution(mesh):
    in_specs = (P("row", "col"), P("row", None), P("row", None))
    out_specs = (P("row", "col"), P("row", "col"))
    return jax.shard_map(
        per_device, mesh=mesh, in_specs=in_specs, out_specs=out_specs, check_vma=False
    )
```

```python
import functools

import jax
import jax.numpy as jnp
from jax import lax
from jax.experimental import pallas as pl
from jax.experimental.pallas import tpu as pltpu
from jax.sharding import PartitionSpec as P

F32, BF16 = jnp.float32, jnp.bfloat16
MESH = pl.DeviceIdType.MESH
NN = (((1,), (0,)), ((), ()))
NT = (((1,), (1,)), ((), ()))
SP = 0
REL = 1
DIR = 1
TP = '01235678'
MP = '2345789a'
HS = '1'
HQ = '5'
HF = '6'
HG = 'a'
S = 32
PIECE = 64
T = 16
G = 128


def split(a):
    hi = a.astype(BF16)
    return hi, (a - hi.astype(F32)).astype(BF16)


def dot3(a, b, dims):
    ah, al = a
    bh, bl = b
    dot = functools.partial(lax.dot_general, dimension_numbers=dims, preferred_element_type=F32)
    return dot(ah, bh) + (dot(ah, bl) + dot(al, bh))


def kernel(
    c_ref, z_ref, h_ref, dc_ref, dz_ref,
    cv, hv, zfirst, zown, zslab, zsub, zct, hc, m, relay, ch, cl, th, tl, pt, ra, sb, rb, rt, tt, rc, se, rd, tot, dzt,
    send, rsend, in_sem,
    st_sem, h_sem, m_sem, y_sem, zg_sem, zc_sem, hg_sem, hcs_sem, ra_sem, rb_sem, ag_sem, rc_sem, rd_sem, fin_sem,
):
    r, c = lax.axis_index("row"), lax.axis_index("col")
    y, zl, co = r // 4, (r // 2) % 2, r % 2
    x, zh = c // 4, c % 4
    swap = r != c
    diagonal = x == y if REL else x > 99
    far = (x - y + 4) % 4 == 2 if REL else x > 99
    near = jnp.logical_and(swap, jnp.logical_not(far))
    mate = r + 1 - 2 * co
    turn = (x + y) % 4

    def rows(start, size):
        return pl.ds(pl.multiple_of(start * size, size), size)

    def share(start):
        return rows(start, T)

    def row_peer(dy, dz):
        return ((y + dy) % 4) * 4 + ((zl + dz) % 2) * 2 + co

    def slice_from(dy, dz, core):
        return ((y - dy + x + 4) % 4) * 4 + ((zl + dz) % 2) * 2 + core

    count = [0]
    pending = []

    def copy(src, dst, sem, row, col):
        n = count[0]
        count[0] += 1
        return pltpu.make_async_remote_copy(
            src_ref=src, dst_ref=dst, send_sem=send.at[n], recv_sem=sem,
            device_id={"row": row, "col": col}, device_id_type=MESH,
        )

    def put(src, dst, sem, row, col):
        one = copy(src, dst, sem, row, col)
        one.start()
        pending.append((None, one))

    def put_if(where, src, dst, sem, row, col):
        one = copy(src, dst, sem, row, col)

        @pl.when(where)
        def _():
            one.start()

        pending.append((where, one))

    def got(dst, sem):
        pltpu.make_async_remote_copy(
            src_ref=dst, dst_ref=dst, send_sem=rsend, recv_sem=sem,
            device_id={"row": mate, "col": c}, device_id_type=MESH,
        ).wait_recv()

    def got_if(where, dst, sem):
        @pl.when(where)
        def _():
            got(dst, sem)

    lanes = lambda k: pl.ds(pl.multiple_of(k * G, G), G)
    loads = [
        pltpu.make_async_copy(z_ref.at[:, lanes(turn)], zfirst, in_sem.at[0]),
        pltpu.make_async_copy(c_ref, cv, in_sem.at[1]),
        pltpu.make_async_copy(z_ref.at[:, lanes(x)], zown, in_sem.at[2]),
        pltpu.make_async_copy(h_ref, hv, in_sem.at[3]),
    ]
    for one in loads:
        one.start()

    barrier = pltpu.get_barrier_semaphore()

    def greet(row, col):
        pl.semaphore_signal(barrier, inc=1, device_id={"row": row, "col": col}, device_id_type=MESH)

    @pl.when(swap)
    def _():
        greet(c, r)

    @pl.when(diagonal)
    def _():
        greet(((y + 2) % 4) * 4 + zh, r)

    peers = [(mate, c)]
    peers += [(row_peer(dy, dz), c) for dy in range(4) for dz in range(2) if dy or dz]
    peers += [(r, ((x + d) % 4) * 4 + zh) for d in range(1, 4)]
    peers += [(r, x * 4 + (zh + d) % 4) for d in range(1, 4)]
    for row, col in peers:
        greet(row, col)
    loads[0].wait()
    zslab[...] = zfirst[...].T
    pl.semaphore_wait(barrier, len(peers) + swap.astype(jnp.int32) + far.astype(jnp.int32))

    mine = turn * 4 + zh
    for h in range(2):
        put_if(swap, zslab.at[share(zh * 2 + h)], zct.at[h, share(mine)], st_sem.at[h], c, r)

        @pl.when(jnp.logical_not(swap))
        def _(h=h):
            zct[h, share(mine)] = zslab[share(zh * 2 + h)]

    def mirror_out(i):
        part = pl.ds(i * PIECE, PIECE)
        put_if(near, c_ref.at[part], m.at[part], m_sem.at[i], c, r)
        put_if(far, c_ref.at[part], relay.at[part], y_sem.at[i], c, x * 4 + r % 4)

    def mirror_pass(i):
        part = pl.ds(i * PIECE, PIECE)
        got_if(diagonal, relay.at[part], y_sem.at[i])
        put_if(diagonal, relay.at[part], m.at[part], m_sem.at[i], r, ((y + 2) % 4) * 4 + zh)

    def spread(at, own, across, direct=False):
        here = at(slice_from(0, 0, co))
        put(here, here, across.at[0, 0], mate, c)
        put(here, here, own.at[0, 1], row_peer(0, 1), c)
        for dy in (1, 3, 2):
            put(here, here, own.at[dy, 0], row_peer(dy, 0), c)
        if direct:
            for dy in (1, 3, 2):
                put(here, here, own.at[dy, 1], row_peer(dy, 1), c)

    def forward(at, own, across, dy, dz, direct=False):
        here = at(slice_from(dy, dz, co))
        got(here, own.at[dy, dz])
        put(here, here, across.at[dy, dz], mate, c)
        if dy == 0 and not direct:
            for to in (1, 3, 2):
                put(here, here, own.at[to, 1], row_peer(to, 0), c)

    def collect(at, across, dy):
        for dz in range(2):
            got(at(slice_from(dy, dz, 1 - co)), across.at[dy, dz])

    factor = lambda s: hc.at[rows(s, S)]
    feature = [lambda s, h=h: zct.at[h, share(s)] for h in range(2)]

    def point(name):
        if name == HS:
            put_if(swap, h_ref.at[rows(mine, S)], hc.at[rows(mine, S)], h_sem, c, r)
        if name == HQ:
            got_if(swap, hc.at[rows(mine, S)], h_sem)
            spread(factor, hg_sem, hcs_sem)
        if name == HF:
            forward(factor, hg_sem, hcs_sem, 0, 1)
        if name == HG:
            for dy, dz in ((1, 0), (3, 0), (2, 0), (1, 1), (3, 1), (2, 1)):
                forward(factor, hg_sem, hcs_sem, dy, dz)
        for i in range(8):
            if TP[i] == name:
                mirror_out(i)
        for i in range(8):
            if MP[i] == name:
                mirror_pass(i)

    point("0")
    loads[1].wait()
    hi, lo = split(cv[...])
    ch[...] = hi
    cl[...] = lo
    hi, lo = split(cv[...].T)
    th[...] = hi
    tl[...] = lo
    loads[2].wait()
    zsub[...] = zown[...].T
    loads[3].wait()

    @pl.when(jnp.logical_not(swap))
    def _():
        hc[rows(mine, S)] = hv[rows(mine, S)]

    def begin(h):
        got_if(swap, zct.at[h, share(mine)], st_sem.at[h])
        spread(feature[h], zg_sem.at[h], zc_sem.at[h], h < DIR)

    begin(0)
    if SP == 0:
        begin(1)
    point("1")

    def product(h, step, dy):
        collect(feature[h], zc_sem.at[h], dy)
        k = (y - dy + x + 4) % 4
        pt[h, step] = dot3(split(zct[h, rows(k, 4 * T)]), (th[...], tl[...]), NN)
        for j in (1, 2, 3, 0):
            zj = (zh + j) % 4
            put_if(k != x, pt.at[h, step, share(zj)], ra.at[h, x, share(zj)], ra_sem.at[h, x, j], r, k * 4 + zh)

        @pl.when(k == x)
        def _():
            ra[h, x] = pt[h, step]

    def products(h):
        pair = feature[h], zg_sem.at[h], zc_sem.at[h]
        forward(*pair, 0, 1, h < DIR)
        if h == 0 and SP == 1:
            begin(1)
        product(h, 0, 0)
        for dy, dz in ((1, 0), (3, 0), (1, 1), (3, 1)):
            forward(*pair, dy, dz)
        if h == 0 and SP == 2:
            begin(1)
        product(h, 1, 1 + 2 * co)
        product(h, 2, 3 - 2 * co)
        point("24"[h])
        for dz in range(2):
            forward(*pair, 2, dz)
        if h == 0 and SP == 3:
            begin(1)
        product(h, 3, 2)
        point("35"[h])

    def sum_x(h):
        for j in (1, 2, 3, 0):
            zj = (zh + j) % 4
            for d in range(1, 4):
                source = (x + d) % 4
                got(ra.at[h, source, share(zj)], ra_sem.at[h, source, j])
            at = share(zj)
            sb[h, j] = (ra[h, 0, at] + ra[h, 1, at]) + (ra[h, 2, at] + ra[h, 3, at])
            if j:
                put(sb.at[h, j], rb.at[h, j], rb_sem.at[h, j], r, x * 4 + zj)

    def sum_z(h):
        for j in range(1, 4):
            got(rb.at[h, j], rb_sem.at[h, j])
        rt[h, share(c)] = sb[h, 0] + rb[h, 1] + rb[h, 2] + rb[h, 3] - zsub[share(zh * 2 + h)]
        own = rt.at[h, share(c)]
        for j in range(1, 4):
            put(own, own, ag_sem.at[h, 0, j], r, x * 4 + (zh + j) % 4)
        for d in (1, 3, 2):
            put(own, own, ag_sem.at[h, d, 0], r, ((x + d) % 4) * 4 + zh)

    def spread_x(h):
        for j in range(1, 4):
            here = rt.at[h, share(x * 4 + (zh - j + 4) % 4)]
            got(here, ag_sem.at[h, 0, j])
            for d in (1, 3, 2):
                put(here, here, ag_sem.at[h, d, j], r, ((x + d) % 4) * 4 + zh)

    products(0)
    products(1)
    sum_x(0)
    sum_z(0)
    point("6")
    sum_x(1)
    spread_x(0)
    point("7")
    sum_z(1)
    spread_x(1)
    point("8")

    slot = y * 2 + zl

    def term(h, d):
        k = (x - d + 4) % 4
        if d:
            for j in range(4):
                got(rt.at[h, share(k * 4 + (zh - j + 4) % 4)], ag_sem.at[h, d, j])
        tt[h, d] = dot3(split(rt[h, rows(k, 4 * T)]), (ch[...], cl[...]), NN)
        for j in range(2):
            put(tt.at[h, d, share(j * 2 + 1 - co)], rc.at[h, d, j], rc_sem.at[h, d, j], mate, c)

    def sum_core(h, d):
        k = (x - d + 4) % 4
        for j in range(2):
            got(rc.at[h, d, j], rc_sem.at[h, d, j])
            target = k * 4 + j * 2 + co
            se[h, d, j] = tt[h, d, share(j * 2 + co)] + rc[h, d, j]
            put_if(target != r, se.at[h, d, j], rd.at[h, slot], rd_sem.at[h, slot], target, c)

            @pl.when(target == r)
            def _():
                rd[h, slot] = se[h, d, j]

    def sum_row(h):
        for s in range(8):
            got_if(s != slot, rd.at[h, s], rd_sem.at[h, s])
        tot[h] = ((rd[h, 0] + rd[h, 1]) + (rd[h, 2] + rd[h, 3])) + ((rd[h, 4] + rd[h, 5]) + (rd[h, 6] + rd[h, 7]))
        put_if(swap, tot.at[h], dzt.at[share(h)], fin_sem.at[h], c, r)

        @pl.when(jnp.logical_not(swap))
        def _():
            dzt[share(h)] = tot[h]

    term(0, 0)
    term(1, 0)
    sum_core(0, 0)
    sum_core(1, 0)
    for h in range(2):
        for d in (1, 3, 2):
            term(h, d)
        for d in (1, 3, 2):
            sum_core(h, d)
        point("9a"[h])
    sum_row(0)
    point("b")
    sum_row(1)
    point("c")
    for dy in range(4):
        collect(factor, hcs_sem, dy)
    own_c = cv[...]
    dc_ref[...] = own_c * own_c - 2.0 * dot3(split(hv[...]), split(hc[...]), NT)
    outer = dot3(split(rt[0].T), split(zct[0]), NN) + dot3(split(rt[1].T), split(zct[1]), NN)
    dc_ref[...] = outer + cv[...] * dc_ref[...]

    for i in range(8):
        got_if(swap, m.at[pl.ds(i * PIECE, PIECE)], m_sem.at[i])

    @pl.when(jnp.logical_not(swap))
    def _():
        m[...] = cv[...]

    across = m[...].T
    dc_ref[...] += cv[...] * (across * across)

    for h in range(2):
        got_if(swap, dzt.at[share(h)], fin_sem.at[h])
        rs = rt[h, share(c)]
        dzt[share(h)] = dzt[share(h)] - rs
    dz_ref[...] = dzt[...].T

    for where, one in pending:
        if where is None:
            one.wait_send()
        else:

            @pl.when(where)
            def _(one=one):
                one.wait_send()


def per_device(coeffs, features, factors):
    n, f = features.shape
    k = factors.shape[1]
    vmem = pl.BlockSpec(memory_space=pltpu.VMEM)
    dma = pltpu.SemaphoreType.DMA
    buf = lambda *shape: pltpu.VMEM(shape, F32)
    half = lambda *shape: pltpu.VMEM(shape, BF16)
    return pl.pallas_call(
        kernel,
        out_shape=(
            jax.ShapeDtypeStruct((n, n), F32),
            jax.ShapeDtypeStruct((n, S), F32),
        ),
        in_specs=[pl.BlockSpec(memory_space=pl.ANY)] * 3,
        out_specs=(vmem, vmem),
        scratch_shapes=[
            buf(n, n), buf(n, k), buf(n, G), buf(n, G), buf(G, n), buf(G, n), buf(2, f // 2, n), buf(n, k),
            buf(n, n), buf(n, n), half(n, n), half(n, n), half(n, n), half(n, n),
            buf(2, 4, 4 * T, n), buf(2, 4, 4 * T, n), buf(2, 4, T, n), buf(2, 4, T, n), buf(2, f // 2, n),
            buf(2, 4, 4 * T, n), buf(2, 4, 2, T, n), buf(2, 4, 2, T, n), buf(2, 8, T, n), buf(2, T, n), buf(S, n),
            dma((192,)), dma(()), dma((4,)),
            dma((2,)), dma(()), dma((8,)), dma((8,)), dma((2, 4, 2)), dma((2, 4, 2)), dma((4, 2)), dma((4, 2)),
            dma((2, 4, 4)), dma((2, 4)), dma((2, 4, 4)), dma((2, 4, 2)), dma((2, 8)), dma((2,)),
        ],
        compiler_params=pltpu.CompilerParams(
            collective_id=0, has_side_effects=True, vmem_limit_bytes=48 << 20
        ),
    )(coeffs, features, factors)


def solution(mesh):
    in_specs = (P("row", "col"), P("row", None), P("row", None))
    out_specs = (P("row", "col"), P("row", "col"))
    return jax.shard_map(
        per_device, mesh=mesh, in_specs=in_specs, out_specs=out_specs, check_vma=False
    )
```

```python
import functools

import jax
import jax.numpy as jnp
from jax import lax
from jax.experimental import pallas as pl
from jax.experimental.pallas import tpu as pltpu
from jax.sharding import PartitionSpec as P

F32, BF16 = jnp.float32, jnp.bfloat16
MESH = pl.DeviceIdType.MESH
NN = (((1,), (0,)), ((), ()))
NT = (((1,), (1,)), ((), ()))
TF = '01235678'
XF = 1
SP = 0
REL = 1
DIR = 1
TP = '01235679'
MP = '2345789a'
HS = '1'
HQ = '6'
HF = '7'
HG = 'a'
S = 32
PIECE = 64
XO = (2, 1, 3) if XF else (1, 3, 2)
T = 16
G = 128


def split(a):
    hi = a.astype(BF16)
    return hi, (a - hi.astype(F32)).astype(BF16)


def dot3(a, b, dims):
    ah, al = a
    bh, bl = b
    dot = functools.partial(lax.dot_general, dimension_numbers=dims, preferred_element_type=F32)
    return dot(ah, bh) + (dot(ah, bl) + dot(al, bh))


def kernel(
    c_ref, z_ref, h_ref, dc_ref, dz_ref,
    cv, hv, zfirst, zown, zslab, zsub, zct, hc, m, relay, ch, cl, th, tl, pt, ra, sb, rb, rt, tt, rc, se, rd, tot, dzt,
    send, rsend, in_sem,
    st_sem, h_sem, m_sem, y_sem, zg_sem, zc_sem, hg_sem, hcs_sem, ra_sem, rb_sem, ag_sem, rc_sem, rd_sem, fin_sem,
):
    r, c = lax.axis_index("row"), lax.axis_index("col")
    y, zl, co = r // 4, (r // 2) % 2, r % 2
    x, zh = c // 4, c % 4
    swap = r != c
    diagonal = x == y if REL else x > 99
    far = (x - y + 4) % 4 == 2 if REL else x > 99
    near = jnp.logical_and(swap, jnp.logical_not(far))
    mate = r + 1 - 2 * co
    turn = (x + y) % 4

    def rows(start, size):
        return pl.ds(pl.multiple_of(start * size, size), size)

    def share(start):
        return rows(start, T)

    def row_peer(dy, dz):
        return ((y + dy) % 4) * 4 + ((zl + dz) % 2) * 2 + co

    def slice_from(dy, dz, core):
        return ((y - dy + x + 4) % 4) * 4 + ((zl + dz) % 2) * 2 + core

    count = [0]
    pending = []

    def copy(src, dst, sem, row, col):
        n = count[0]
        count[0] += 1
        return pltpu.make_async_remote_copy(
            src_ref=src, dst_ref=dst, send_sem=send.at[n], recv_sem=sem,
            device_id={"row": row, "col": col}, device_id_type=MESH,
        )

    def put(src, dst, sem, row, col):
        one = copy(src, dst, sem, row, col)
        one.start()
        pending.append((None, one))

    def put_if(where, src, dst, sem, row, col):
        one = copy(src, dst, sem, row, col)

        @pl.when(where)
        def _():
            one.start()

        pending.append((where, one))

    def got(dst, sem):
        pltpu.make_async_remote_copy(
            src_ref=dst, dst_ref=dst, send_sem=rsend, recv_sem=sem,
            device_id={"row": mate, "col": c}, device_id_type=MESH,
        ).wait_recv()

    def got_if(where, dst, sem):
        @pl.when(where)
        def _():
            got(dst, sem)

    lanes = lambda k: pl.ds(pl.multiple_of(k * G, G), G)
    loads = [
        pltpu.make_async_copy(z_ref.at[:, lanes(turn)], zfirst, in_sem.at[0]),
        pltpu.make_async_copy(c_ref, cv, in_sem.at[1]),
        pltpu.make_async_copy(z_ref.at[:, lanes(x)], zown, in_sem.at[2]),
        pltpu.make_async_copy(h_ref, hv, in_sem.at[3]),
    ]
    for one in loads:
        one.start()

    barrier = pltpu.get_barrier_semaphore()

    def greet(row, col):
        pl.semaphore_signal(barrier, inc=1, device_id={"row": row, "col": col}, device_id_type=MESH)

    @pl.when(swap)
    def _():
        greet(c, r)

    @pl.when(diagonal)
    def _():
        greet(((y + 2) % 4) * 4 + zh, r)

    peers = [(mate, c)]
    peers += [(row_peer(dy, dz), c) for dy in range(4) for dz in range(2) if dy or dz]
    peers += [(r, ((x + d) % 4) * 4 + zh) for d in range(1, 4)]
    peers += [(r, x * 4 + (zh + d) % 4) for d in range(1, 4)]
    for row, col in peers:
        greet(row, col)
    loads[0].wait()
    zslab[...] = zfirst[...].T
    pl.semaphore_wait(barrier, len(peers) + swap.astype(jnp.int32) + far.astype(jnp.int32))

    mine = turn * 4 + zh
    for h in range(2):
        put_if(swap, zslab.at[share(zh * 2 + h)], zct.at[h, share(mine)], st_sem.at[h], c, r)

        @pl.when(jnp.logical_not(swap))
        def _(h=h):
            zct[h, share(mine)] = zslab[share(zh * 2 + h)]

    def mirror_out(i):
        part = pl.ds(i * PIECE, PIECE)
        put_if(near, c_ref.at[part], m.at[part], m_sem.at[i], c, r)

    def mirror_far(i):
        part = pl.ds(i * PIECE, PIECE)
        put_if(far, c_ref.at[part], relay.at[part], y_sem.at[i], c, x * 4 + r % 4)

    def mirror_pass(i):
        part = pl.ds(i * PIECE, PIECE)
        got_if(diagonal, relay.at[part], y_sem.at[i])
        put_if(diagonal, relay.at[part], m.at[part], m_sem.at[i], r, ((y + 2) % 4) * 4 + zh)

    def spread(at, own, across, direct=False):
        here = at(slice_from(0, 0, co))
        put(here, here, across.at[0, 0], mate, c)
        put(here, here, own.at[0, 1], row_peer(0, 1), c)
        for dy in (1, 3, 2):
            put(here, here, own.at[dy, 0], row_peer(dy, 0), c)
        if direct:
            for dy in (1, 3, 2):
                put(here, here, own.at[dy, 1], row_peer(dy, 1), c)

    def forward(at, own, across, dy, dz, direct=False):
        here = at(slice_from(dy, dz, co))
        got(here, own.at[dy, dz])
        put(here, here, across.at[dy, dz], mate, c)
        if dy == 0 and not direct:
            for to in (1, 3, 2):
                put(here, here, own.at[to, 1], row_peer(to, 0), c)

    def collect(at, across, dy):
        for dz in range(2):
            got(at(slice_from(dy, dz, 1 - co)), across.at[dy, dz])

    factor = lambda s: hc.at[rows(s, S)]
    feature = [lambda s, h=h: zct.at[h, share(s)] for h in range(2)]

    def point(name):
        if name == HS:
            put_if(swap, h_ref.at[rows(mine, S)], hc.at[rows(mine, S)], h_sem, c, r)
        if name == HQ:
            got_if(swap, hc.at[rows(mine, S)], h_sem)
            spread(factor, hg_sem, hcs_sem)
        if name == HF:
            forward(factor, hg_sem, hcs_sem, 0, 1)
        if name == HG:
            for dy, dz in ((1, 0), (3, 0), (2, 0), (1, 1), (3, 1), (2, 1)):
                forward(factor, hg_sem, hcs_sem, dy, dz)
        for i in range(8):
            if TP[i] == name:
                mirror_out(i)
        for i in range(8):
            if TF[i] == name:
                mirror_far(i)
        for i in range(8):
            if MP[i] == name:
                mirror_pass(i)

    point("0")
    loads[1].wait()
    hi, lo = split(cv[...])
    ch[...] = hi
    cl[...] = lo
    hi, lo = split(cv[...].T)
    th[...] = hi
    tl[...] = lo
    loads[2].wait()
    zsub[...] = zown[...].T
    loads[3].wait()

    @pl.when(jnp.logical_not(swap))
    def _():
        hc[rows(mine, S)] = hv[rows(mine, S)]

    def begin(h):
        got_if(swap, zct.at[h, share(mine)], st_sem.at[h])
        spread(feature[h], zg_sem.at[h], zc_sem.at[h], h < DIR)

    begin(0)
    if SP == 0:
        begin(1)
    point("1")

    def product(h, step, dy):
        collect(feature[h], zc_sem.at[h], dy)
        k = (y - dy + x + 4) % 4
        pt[h, step] = dot3(split(zct[h, rows(k, 4 * T)]), (th[...], tl[...]), NN)
        for j in (1, 2, 3, 0):
            zj = (zh + j) % 4
            put_if(k != x, pt.at[h, step, share(zj)], ra.at[h, x, share(zj)], ra_sem.at[h, x, j], r, k * 4 + zh)

        @pl.when(k == x)
        def _():
            ra[h, x] = pt[h, step]

    def products(h):
        pair = feature[h], zg_sem.at[h], zc_sem.at[h]
        forward(*pair, 0, 1, h < DIR)
        if h == 0 and SP == 1:
            begin(1)
        product(h, 0, 0)
        for dy, dz in ((1, 0), (3, 0), (1, 1), (3, 1)):
            forward(*pair, dy, dz)
        if h == 0 and SP == 2:
            begin(1)
        product(h, 1, 1 + 2 * co)
        product(h, 2, 3 - 2 * co)
        point("24"[h])
        for dz in range(2):
            forward(*pair, 2, dz)
        if h == 0 and SP == 3:
            begin(1)
        product(h, 3, 2)
        point("35"[h])

    def sum_x(h):
        for j in (1, 2, 3, 0):
            zj = (zh + j) % 4
            for d in range(1, 4):
                source = (x + d) % 4
                got(ra.at[h, source, share(zj)], ra_sem.at[h, source, j])
            at = share(zj)
            sb[h, j] = (ra[h, 0, at] + ra[h, 1, at]) + (ra[h, 2, at] + ra[h, 3, at])
            if j:
                put(sb.at[h, j], rb.at[h, j], rb_sem.at[h, j], r, x * 4 + zj)

    def sum_z(h):
        for j in range(1, 4):
            got(rb.at[h, j], rb_sem.at[h, j])
        rt[h, share(c)] = sb[h, 0] + rb[h, 1] + rb[h, 2] + rb[h, 3] - zsub[share(zh * 2 + h)]
        own = rt.at[h, share(c)]
        for j in range(1, 4):
            put(own, own, ag_sem.at[h, 0, j], r, x * 4 + (zh + j) % 4)
        for d in XO:
            put(own, own, ag_sem.at[h, d, 0], r, ((x + d) % 4) * 4 + zh)

    def spread_x(h):
        for j in range(1, 4):
            here = rt.at[h, share(x * 4 + (zh - j + 4) % 4)]
            got(here, ag_sem.at[h, 0, j])
            for d in XO:
                put(here, here, ag_sem.at[h, d, j], r, ((x + d) % 4) * 4 + zh)

    products(0)
    products(1)
    sum_x(0)
    sum_z(0)
    point("6")
    sum_x(1)
    spread_x(0)
    point("7")
    sum_z(1)
    spread_x(1)
    point("8")

    slot = y * 2 + zl

    def term(h, d):
        k = (x - d + 4) % 4
        if d:
            for j in range(4):
                got(rt.at[h, share(k * 4 + (zh - j + 4) % 4)], ag_sem.at[h, d, j])
        tt[h, d] = dot3(split(rt[h, rows(k, 4 * T)]), (ch[...], cl[...]), NN)
        for j in range(2):
            put(tt.at[h, d, share(j * 2 + 1 - co)], rc.at[h, d, j], rc_sem.at[h, d, j], mate, c)

    def sum_core(h, d):
        k = (x - d + 4) % 4
        for j in range(2):
            got(rc.at[h, d, j], rc_sem.at[h, d, j])
            target = k * 4 + j * 2 + co
            se[h, d, j] = tt[h, d, share(j * 2 + co)] + rc[h, d, j]
            put_if(target != r, se.at[h, d, j], rd.at[h, slot], rd_sem.at[h, slot], target, c)

            @pl.when(target == r)
            def _():
                rd[h, slot] = se[h, d, j]

    def sum_row(h):
        for s in range(8):
            got_if(s != slot, rd.at[h, s], rd_sem.at[h, s])
        tot[h] = ((rd[h, 0] + rd[h, 1]) + (rd[h, 2] + rd[h, 3])) + ((rd[h, 4] + rd[h, 5]) + (rd[h, 6] + rd[h, 7]))
        put_if(swap, tot.at[h], dzt.at[share(h)], fin_sem.at[h], c, r)

        @pl.when(jnp.logical_not(swap))
        def _():
            dzt[share(h)] = tot[h]

    term(0, 0)
    term(1, 0)
    sum_core(0, 0)
    sum_core(1, 0)
    for h in range(2):
        for d in (1, 3, 2):
            term(h, d)
        for d in (1, 3, 2):
            sum_core(h, d)
        point("9a"[h])
    sum_row(0)
    point("b")
    sum_row(1)
    point("c")
    for dy in range(4):
        collect(factor, hcs_sem, dy)
    own_c = cv[...]
    dc_ref[...] = own_c * own_c - 2.0 * dot3(split(hv[...]), split(hc[...]), NT)
    outer = dot3(split(rt[0].T), split(zct[0]), NN) + dot3(split(rt[1].T), split(zct[1]), NN)
    dc_ref[...] = outer + cv[...] * dc_ref[...]

    for i in range(8):
        got_if(swap, m.at[pl.ds(i * PIECE, PIECE)], m_sem.at[i])

    @pl.when(jnp.logical_not(swap))
    def _():
        m[...] = cv[...]

    across = m[...].T
    dc_ref[...] += cv[...] * (across * across)

    for h in range(2):
        got_if(swap, dzt.at[share(h)], fin_sem.at[h])
        rs = rt[h, share(c)]
        dzt[share(h)] = dzt[share(h)] - rs
    dz_ref[...] = dzt[...].T

    for where, one in pending:
        if where is None:
            one.wait_send()
        else:

            @pl.when(where)
            def _(one=one):
                one.wait_send()


def per_device(coeffs, features, factors):
    n, f = features.shape
    k = factors.shape[1]
    vmem = pl.BlockSpec(memory_space=pltpu.VMEM)
    dma = pltpu.SemaphoreType.DMA
    buf = lambda *shape: pltpu.VMEM(shape, F32)
    half = lambda *shape: pltpu.VMEM(shape, BF16)
    return pl.pallas_call(
        kernel,
        out_shape=(
            jax.ShapeDtypeStruct((n, n), F32),
            jax.ShapeDtypeStruct((n, S), F32),
        ),
        in_specs=[pl.BlockSpec(memory_space=pl.ANY)] * 3,
        out_specs=(vmem, vmem),
        scratch_shapes=[
            buf(n, n), buf(n, k), buf(n, G), buf(n, G), buf(G, n), buf(G, n), buf(2, f // 2, n), buf(n, k),
            buf(n, n), buf(n, n), half(n, n), half(n, n), half(n, n), half(n, n),
            buf(2, 4, 4 * T, n), buf(2, 4, 4 * T, n), buf(2, 4, T, n), buf(2, 4, T, n), buf(2, f // 2, n),
            buf(2, 4, 4 * T, n), buf(2, 4, 2, T, n), buf(2, 4, 2, T, n), buf(2, 8, T, n), buf(2, T, n), buf(S, n),
            dma((192,)), dma(()), dma((4,)),
            dma((2,)), dma(()), dma((8,)), dma((8,)), dma((2, 4, 2)), dma((2, 4, 2)), dma((4, 2)), dma((4, 2)),
            dma((2, 4, 4)), dma((2, 4)), dma((2, 4, 4)), dma((2, 4, 2)), dma((2, 8)), dma((2,)),
        ],
        compiler_params=pltpu.CompilerParams(
            collective_id=0, has_side_effects=True, vmem_limit_bytes=48 << 20
        ),
    )(coeffs, features, factors)


def solution(mesh):
    in_specs = (P("row", "col"), P("row", None), P("row", None))
    out_specs = (P("row", "col"), P("row", "col"))
    return jax.shard_map(
        per_device, mesh=mesh, in_specs=in_specs, out_specs=out_specs, check_vma=False
    )
```

```python
import functools

import jax
import jax.numpy as jnp
from jax import lax
from jax.experimental import pallas as pl
from jax.experimental.pallas import tpu as pltpu
from jax.sharding import PartitionSpec as P

F32, BF16 = jnp.float32, jnp.bfloat16
MESH = pl.DeviceIdType.MESH
NN = (((1,), (0,)), ((), ()))
NT = (((1,), (1,)), ((), ()))
TF = '01235678'
XF = 1
SP = 0
REL = 1
DIR = 1
TP = '01235679'
MP = '2345789a'
HS = '1'
HQ = '6'
HF = '7'
HG = 'b'
S = 32
PIECE = 64
XO = (2, 1, 3) if XF else (1, 3, 2)
T = 16
G = 128


def split(a):
    hi = a.astype(BF16)
    return hi, (a - hi.astype(F32)).astype(BF16)


def dot3(a, b, dims):
    ah, al = a
    bh, bl = b
    dot = functools.partial(lax.dot_general, dimension_numbers=dims, preferred_element_type=F32)
    return dot(ah, bh) + (dot(ah, bl) + dot(al, bh))


def kernel(
    c_ref, z_ref, h_ref, dc_ref, dz_ref,
    cv, hv, zfirst, zown, zslab, zsub, zct, hc, m, relay, ch, cl, th, tl, pt, ra, sb, rb, rt, tt, rc, se, rd, tot, dzt,
    send, rsend, in_sem,
    st_sem, h_sem, m_sem, y_sem, zg_sem, zc_sem, hg_sem, hcs_sem, ra_sem, rb_sem, ag_sem, rc_sem, rd_sem, fin_sem,
):
    r, c = lax.axis_index("row"), lax.axis_index("col")
    y, zl, co = r // 4, (r // 2) % 2, r % 2
    x, zh = c // 4, c % 4
    swap = r != c
    diagonal = x == y if REL else x > 99
    far = (x - y + 4) % 4 == 2 if REL else x > 99
    near = jnp.logical_and(swap, jnp.logical_not(far))
    mate = r + 1 - 2 * co
    turn = (x + y) % 4

    def rows(start, size):
        return pl.ds(pl.multiple_of(start * size, size), size)

    def share(start):
        return rows(start, T)

    def row_peer(dy, dz):
        return ((y + dy) % 4) * 4 + ((zl + dz) % 2) * 2 + co

    def slice_from(dy, dz, core):
        return ((y - dy + x + 4) % 4) * 4 + ((zl + dz) % 2) * 2 + core

    count = [0]
    pending = []

    def copy(src, dst, sem, row, col):
        n = count[0]
        count[0] += 1
        return pltpu.make_async_remote_copy(
            src_ref=src, dst_ref=dst, send_sem=send.at[n], recv_sem=sem,
            device_id={"row": row, "col": col}, device_id_type=MESH,
        )

    def put(src, dst, sem, row, col):
        one = copy(src, dst, sem, row, col)
        one.start()
        pending.append((None, one))

    def put_if(where, src, dst, sem, row, col):
        one = copy(src, dst, sem, row, col)

        @pl.when(where)
        def _():
            one.start()

        pending.append((where, one))

    def got(dst, sem):
        pltpu.make_async_remote_copy(
            src_ref=dst, dst_ref=dst, send_sem=rsend, recv_sem=sem,
            device_id={"row": mate, "col": c}, device_id_type=MESH,
        ).wait_recv()

    def got_if(where, dst, sem):
        @pl.when(where)
        def _():
            got(dst, sem)

    lanes = lambda k: pl.ds(pl.multiple_of(k * G, G), G)
    loads = [
        pltpu.make_async_copy(z_ref.at[:, lanes(turn)], zfirst, in_sem.at[0]),
        pltpu.make_async_copy(c_ref, cv, in_sem.at[1]),
        pltpu.make_async_copy(z_ref.at[:, lanes(x)], zown, in_sem.at[2]),
        pltpu.make_async_copy(h_ref, hv, in_sem.at[3]),
    ]
    for one in loads:
        one.start()

    barrier = pltpu.get_barrier_semaphore()

    def greet(row, col):
        pl.semaphore_signal(barrier, inc=1, device_id={"row": row, "col": col}, device_id_type=MESH)

    @pl.when(swap)
    def _():
        greet(c, r)

    @pl.when(diagonal)
    def _():
        greet(((y + 2) % 4) * 4 + zh, r)

    peers = [(mate, c)]
    peers += [(row_peer(dy, dz), c) for dy in range(4) for dz in range(2) if dy or dz]
    peers += [(r, ((x + d) % 4) * 4 + zh) for d in range(1, 4)]
    peers += [(r, x * 4 + (zh + d) % 4) for d in range(1, 4)]
    for row, col in peers:
        greet(row, col)
    loads[0].wait()
    zslab[...] = zfirst[...].T
    pl.semaphore_wait(barrier, len(peers) + swap.astype(jnp.int32) + far.astype(jnp.int32))

    mine = turn * 4 + zh
    for h in range(2):
        put_if(swap, zslab.at[share(zh * 2 + h)], zct.at[h, share(mine)], st_sem.at[h], c, r)

        @pl.when(jnp.logical_not(swap))
        def _(h=h):
            zct[h, share(mine)] = zslab[share(zh * 2 + h)]

    def mirror_out(i):
        part = pl.ds(i * PIECE, PIECE)
        put_if(near, c_ref.at[part], m.at[part], m_sem.at[i], c, r)

    def mirror_far(i):
        part = pl.ds(i * PIECE, PIECE)
        put_if(far, c_ref.at[part], relay.at[part], y_sem.at[i], c, x * 4 + r % 4)

    def mirror_pass(i):
        part = pl.ds(i * PIECE, PIECE)
        got_if(diagonal, relay.at[part], y_sem.at[i])
        put_if(diagonal, relay.at[part], m.at[part], m_sem.at[i], r, ((y + 2) % 4) * 4 + zh)

    def spread(at, own, across, direct=False):
        here = at(slice_from(0, 0, co))
        put(here, here, across.at[0, 0], mate, c)
        put(here, here, own.at[0, 1], row_peer(0, 1), c)
        for dy in (1, 3, 2):
            put(here, here, own.at[dy, 0], row_peer(dy, 0), c)
        if direct:
            for dy in (1, 3, 2):
                put(here, here, own.at[dy, 1], row_peer(dy, 1), c)

    def forward(at, own, across, dy, dz, direct=False):
        here = at(slice_from(dy, dz, co))
        got(here, own.at[dy, dz])
        put(here, here, across.at[dy, dz], mate, c)
        if dy == 0 and not direct:
            for to in (1, 3, 2):
                put(here, here, own.at[to, 1], row_peer(to, 0), c)

    def collect(at, across, dy):
        for dz in range(2):
            got(at(slice_from(dy, dz, 1 - co)), across.at[dy, dz])

    factor = lambda s: hc.at[rows(s, S)]
    feature = [lambda s, h=h: zct.at[h, share(s)] for h in range(2)]

    def point(name):
        if name == HS:
            put_if(swap, h_ref.at[rows(mine, S)], hc.at[rows(mine, S)], h_sem, c, r)
        if name == HQ:
            got_if(swap, hc.at[rows(mine, S)], h_sem)
            spread(factor, hg_sem, hcs_sem)
        if name == HF:
            forward(factor, hg_sem, hcs_sem, 0, 1)
        if name == HG:
            for dy, dz in ((1, 0), (3, 0), (2, 0), (1, 1), (3, 1), (2, 1)):
                forward(factor, hg_sem, hcs_sem, dy, dz)
        for i in range(8):
            if TP[i] == name:
                mirror_out(i)
        for i in range(8):
            if TF[i] == name:
                mirror_far(i)
        for i in range(8):
            if MP[i] == name:
                mirror_pass(i)

    point("0")
    loads[1].wait()
    hi, lo = split(cv[...])
    ch[...] = hi
    cl[...] = lo
    hi, lo = split(cv[...].T)
    th[...] = hi
    tl[...] = lo
    loads[2].wait()
    zsub[...] = zown[...].T
    loads[3].wait()

    @pl.when(jnp.logical_not(swap))
    def _():
        hc[rows(mine, S)] = hv[rows(mine, S)]

    def begin(h):
        got_if(swap, zct.at[h, share(mine)], st_sem.at[h])
        spread(feature[h], zg_sem.at[h], zc_sem.at[h], h < DIR)

    begin(0)
    if SP == 0:
        begin(1)
    point("1")

    def product(h, step, dy):
        collect(feature[h], zc_sem.at[h], dy)
        k = (y - dy + x + 4) % 4
        pt[h, step] = dot3(split(zct[h, rows(k, 4 * T)]), (th[...], tl[...]), NN)
        for j in (1, 2, 3, 0):
            zj = (zh + j) % 4
            put_if(k != x, pt.at[h, step, share(zj)], ra.at[h, x, share(zj)], ra_sem.at[h, x, j], r, k * 4 + zh)

        @pl.when(k == x)
        def _():
            ra[h, x] = pt[h, step]

    def products(h):
        pair = feature[h], zg_sem.at[h], zc_sem.at[h]
        forward(*pair, 0, 1, h < DIR)
        if h == 0 and SP == 1:
            begin(1)
        product(h, 0, 0)
        for dy, dz in ((1, 0), (3, 0), (1, 1), (3, 1)):
            forward(*pair, dy, dz)
        if h == 0 and SP == 2:
            begin(1)
        product(h, 1, 1 + 2 * co)
        product(h, 2, 3 - 2 * co)
        point("24"[h])
        for dz in range(2):
            forward(*pair, 2, dz)
        if h == 0 and SP == 3:
            begin(1)
        product(h, 3, 2)
        point("35"[h])

    def sum_x(h):
        for j in (1, 2, 3, 0):
            zj = (zh + j) % 4
            for d in range(1, 4):
                source = (x + d) % 4
                got(ra.at[h, source, share(zj)], ra_sem.at[h, source, j])
            at = share(zj)
            sb[h, j] = (ra[h, 0, at] + ra[h, 1, at]) + (ra[h, 2, at] + ra[h, 3, at])
            if j:
                put(sb.at[h, j], rb.at[h, j], rb_sem.at[h, j], r, x * 4 + zj)

    def sum_z(h):
        for j in range(1, 4):
            got(rb.at[h, j], rb_sem.at[h, j])
        rt[h, share(c)] = sb[h, 0] + rb[h, 1] + rb[h, 2] + rb[h, 3] - zsub[share(zh * 2 + h)]
        own = rt.at[h, share(c)]
        for j in range(1, 4):
            put(own, own, ag_sem.at[h, 0, j], r, x * 4 + (zh + j) % 4)
        for d in XO:
            put(own, own, ag_sem.at[h, d, 0], r, ((x + d) % 4) * 4 + zh)

    def spread_x(h):
        for j in range(1, 4):
            here = rt.at[h, share(x * 4 + (zh - j + 4) % 4)]
            got(here, ag_sem.at[h, 0, j])
            for d in XO:
                put(here, here, ag_sem.at[h, d, j], r, ((x + d) % 4) * 4 + zh)

    products(0)
    products(1)
    sum_x(0)
    sum_z(0)
    point("6")
    sum_x(1)
    spread_x(0)
    point("7")
    sum_z(1)
    spread_x(1)
    point("8")

    slot = y * 2 + zl

    def term(h, d):
        k = (x - d + 4) % 4
        if d:
            for j in range(4):
                got(rt.at[h, share(k * 4 + (zh - j + 4) % 4)], ag_sem.at[h, d, j])
        tt[h, d] = dot3(split(rt[h, rows(k, 4 * T)]), (ch[...], cl[...]), NN)
        for j in range(2):
            put(tt.at[h, d, share(j * 2 + 1 - co)], rc.at[h, d, j], rc_sem.at[h, d, j], mate, c)

    def sum_core(h, d):
        k = (x - d + 4) % 4
        for j in range(2):
            got(rc.at[h, d, j], rc_sem.at[h, d, j])
            target = k * 4 + j * 2 + co
            se[h, d, j] = tt[h, d, share(j * 2 + co)] + rc[h, d, j]
            put_if(target != r, se.at[h, d, j], rd.at[h, slot], rd_sem.at[h, slot], target, c)

            @pl.when(target == r)
            def _():
                rd[h, slot] = se[h, d, j]

    def sum_row(h):
        for s in range(8):
            got_if(s != slot, rd.at[h, s], rd_sem.at[h, s])
        tot[h] = ((rd[h, 0] + rd[h, 1]) + (rd[h, 2] + rd[h, 3])) + ((rd[h, 4] + rd[h, 5]) + (rd[h, 6] + rd[h, 7]))
        put_if(swap, tot.at[h], dzt.at[share(h)], fin_sem.at[h], c, r)

        @pl.when(jnp.logical_not(swap))
        def _():
            dzt[share(h)] = tot[h]

    term(0, 0)
    term(1, 0)
    sum_core(0, 0)
    sum_core(1, 0)
    for h in range(2):
        for d in (1, 3, 2):
            term(h, d)
        for d in (1, 3, 2):
            sum_core(h, d)
        point("9a"[h])
    sum_row(0)
    point("b")
    sum_row(1)
    point("c")
    for dy in range(4):
        collect(factor, hcs_sem, dy)
    own_c = cv[...]
    dc_ref[...] = own_c * own_c - 2.0 * dot3(split(hv[...]), split(hc[...]), NT)
    outer = dot3(split(rt[0].T), split(zct[0]), NN) + dot3(split(rt[1].T), split(zct[1]), NN)
    dc_ref[...] = outer + cv[...] * dc_ref[...]

    for i in range(8):
        got_if(swap, m.at[pl.ds(i * PIECE, PIECE)], m_sem.at[i])

    @pl.when(jnp.logical_not(swap))
    def _():
        m[...] = cv[...]

    across = m[...].T
    dc_ref[...] += cv[...] * (across * across)

    for h in range(2):
        got_if(swap, dzt.at[share(h)], fin_sem.at[h])
        rs = rt[h, share(c)]
        dzt[share(h)] = dzt[share(h)] - rs
    dz_ref[...] = dzt[...].T

    for where, one in pending:
        if where is None:
            one.wait_send()
        else:

            @pl.when(where)
            def _(one=one):
                one.wait_send()


def per_device(coeffs, features, factors):
    n, f = features.shape
    k = factors.shape[1]
    vmem = pl.BlockSpec(memory_space=pltpu.VMEM)
    dma = pltpu.SemaphoreType.DMA
    buf = lambda *shape: pltpu.VMEM(shape, F32)
    half = lambda *shape: pltpu.VMEM(shape, BF16)
    return pl.pallas_call(
        kernel,
        out_shape=(
            jax.ShapeDtypeStruct((n, n), F32),
            jax.ShapeDtypeStruct((n, S), F32),
        ),
        in_specs=[pl.BlockSpec(memory_space=pl.ANY)] * 3,
        out_specs=(vmem, vmem),
        scratch_shapes=[
            buf(n, n), buf(n, k), buf(n, G), buf(n, G), buf(G, n), buf(G, n), buf(2, f // 2, n), buf(n, k),
            buf(n, n), buf(n, n), half(n, n), half(n, n), half(n, n), half(n, n),
            buf(2, 4, 4 * T, n), buf(2, 4, 4 * T, n), buf(2, 4, T, n), buf(2, 4, T, n), buf(2, f // 2, n),
            buf(2, 4, 4 * T, n), buf(2, 4, 2, T, n), buf(2, 4, 2, T, n), buf(2, 8, T, n), buf(2, T, n), buf(S, n),
            dma((192,)), dma(()), dma((4,)),
            dma((2,)), dma(()), dma((8,)), dma((8,)), dma((2, 4, 2)), dma((2, 4, 2)), dma((4, 2)), dma((4, 2)),
            dma((2, 4, 4)), dma((2, 4)), dma((2, 4, 4)), dma((2, 4, 2)), dma((2, 8)), dma((2,)),
        ],
        compiler_params=pltpu.CompilerParams(
            collective_id=0, has_side_effects=True, vmem_limit_bytes=48 << 20
        ),
    )(coeffs, features, factors)


def solution(mesh):
    in_specs = (P("row", "col"), P("row", None), P("row", None))
    out_specs = (P("row", "col"), P("row", "col"))
    return jax.shard_map(
        per_device, mesh=mesh, in_specs=in_specs, out_specs=out_specs, check_vma=False
    )
```
